256 devices in a mesh: ctx: 128 (over z_hi, x, y, core), ch: 2 (over z_lo).
Axes of the slice: x: 4, y: 4, z: 8 (z_hi: 4, z_lo: 2; z = z_hi * 2 + z_lo), core: 2. Of those that a mesh axis runs over, the one named last changes fastest.
Arguments:
- activation: bfloat16 [16384, 256], P('ctx', 'ch'), may hold values from -1.5 to 1.5
- cotangent: bfloat16 [16384, 256], P('ctx', 'ch'), may hold values from -6 to 6
- filter_param: bfloat16 [16384, 16], P('ctx', 'ch'), may hold values from -6 to 6
- skip_gain: float32 [256], P('ch'), may hold values from 0.25 to 1.75
Outputs:
- input_grad: bfloat16 [16384, 256], P('ctx', 'ch')
- filter_grad: float32 [16384, 16], P('ctx', 'ch')
The draws below stay inside these ranges and needn't reach their ends.
All inputs are finite; a program needn't handle non-finite values.
Results may differ from the reference program's by a relative error of at most 0.001.
Values may be sent and summed in bfloat16 or wider, within the bound.
No kernel may reach another device: no remote copies, remote signals or barrier semaphores. Data moves between devices by JAX's collectives and lax.ppermute only.
A program may use at most 64 MiB of HBM per device.

```python
import math
import jax
import jax.numpy as jnp
from jax import lax

TOKENS = 16384
CHANNELS = 256
FILTERS = 16


def block_scale(key, dims, cuts, least, largest):
    loudness = 1.0
    for axis_at, parts in cuts:
        draws = jax.random.uniform(jax.random.fold_in(jax.random.fold_in(key, 6), axis_at), (parts,), jnp.float32, least / len(cuts), largest / len(cuts))
        loudness = loudness * jnp.repeat(jnp.exp(draws), dims[axis_at] // parts).reshape((-1,) + (1,) * (len(dims) - 1 - axis_at))
    return loudness


def scatter_about(own_key, extent, spread, most, split=(), dtype=jnp.bfloat16):
    drawn = jax.random.normal(own_key, extent, jnp.float32) * spread
    if len(split) > 0:
        drawn = block_scale(own_key, extent, split, -0.22, 0.18) * drawn
    return jnp.clip(drawn, min=-most, max=most).astype(dtype)


def setup_inputs(seed: int = 0) -> dict:
    arg_keys = jax.random.split(jax.random.key(seed), 5)
    return {
        "activation": scatter_about(arg_keys[0], (TOKENS, CHANNELS), 0.25, 1.5, ((0, 128), (1, 2))),
        "cotangent": scatter_about(arg_keys[1], (TOKENS, CHANNELS), 1.0, 6.0, ((0, 128), (1, 2))),
        "filter_param": scatter_about(arg_keys[2], (TOKENS, FILTERS), 1.0, 6.0, ((0, 128), (1, 2))),
        "skip_gain": jnp.clip(1.0 + 0.15 * jax.random.normal(arg_keys[3], (CHANNELS,), jnp.float32), 0.25, 1.75),
    }


def reference(activation, cotangent, filter_param, skip_gain):
    period = 2 * TOKENS
    scaling = 1.0 / math.sqrt(TOKENS)
    filter_spec = jnp.fft.fft(filter_param.astype(jnp.float32), n=period, axis=0)
    members = CHANNELS // FILTERS
    act_blocks = activation.reshape(TOKENS, members, FILTERS).transpose(1, 0, 2)
    cot_blocks = cotangent.reshape(TOKENS, members, FILTERS).transpose(1, 0, 2)

    def member_step(carry, pieces):
        act_piece, cot_piece = pieces
        act_spec = jnp.fft.fft(act_piece.astype(jnp.float32), n=period, axis=0)
        cot_spec = jnp.fft.fft(cot_piece.astype(jnp.float32), n=period, axis=0)
        conv_term = jnp.real(jnp.fft.ifft(cot_spec * jnp.conj(filter_spec), axis=0))[:TOKENS] * scaling
        product = cot_spec * jnp.conj(act_spec)
        return ((carry[0] + jnp.real(product), carry[1] + jnp.imag(product)), conv_term.astype(jnp.float32))
    start_sums = (jnp.zeros((period, FILTERS), jnp.float32), jnp.zeros((period, FILTERS), jnp.float32))
    (sum_real, sum_imag), conv_terms = lax.scan(member_step, start_sums, (act_blocks, cot_blocks))
    filter_grad = jnp.real(jnp.fft.ifft(sum_real + 1j * sum_imag, axis=0))[:TOKENS] * scaling
    conv_all = conv_terms.transpose(1, 0, 2).reshape(TOKENS, CHANNELS)
    input_grad = (skip_gain[None, :] * cotangent.astype(jnp.float32) + conv_all).astype(jnp.bfloat16)
    return (input_grad, filter_grad.astype(jnp.float32))
```

```python
import jax
import jax.numpy as jnp
from jax import lax
from jax.experimental import pallas as pl
from jax.experimental.pallas import tpu as pltpu
from jax.sharding import PartitionSpec as P

f32 = jnp.float32
bf16 = jnp.bfloat16
B = 128
R = 16
G = B // R


def pack_kernel(act_ref, cot_ref, filt_ref, out_ref, rows):
    here = lax.axis_index("ch")
    at = lax.broadcasted_iota(jnp.int32, (B, B), 0)
    to = lax.broadcasted_iota(jnp.int32, (B, B), 1)
    flip = jnp.where(at + to == B - 1, 1.0, 0.0).astype(bf16)
    cot_t = cot_ref[...].astype(f32).T
    rows[pl.ds(0, B, stride=4), :] = cot_t
    rows[pl.ds(2, B, stride=4), :] = cot_t
    rows[pl.ds(3, B, stride=4), :] = lax.dot_general(
        act_ref[...], flip, (((0,), (0,)), ((), ())), preferred_element_type=f32
    )
    filt = jnp.dot(filt_ref[...], flip, preferred_element_type=f32)
    for h in range(B // 8):
        mine = jnp.where(here == h % 2, filt, 0.0)
        rows[pl.ds(32 * h + 1, 8, stride=4), :] = mine
    out_ref[...] = rows[...].astype(bf16)


def correlate_kernel(in_ref, out_ref, rows, wide, hank, sums, spread):
    here = lax.axis_index("ch")
    rows[...] = in_ref[...].astype(f32)
    q_at = lax.broadcasted_iota(jnp.int32, (B, B), 0)
    b_at = lax.broadcasted_iota(jnp.int32, (B, B), 1)
    inside = b_at <= q_at
    filt = rows[pl.ds(1, B, stride=4), :] + rows[pl.ds(3, B, stride=4), :]
    results = []
    for half in range(2):
        weight = jnp.where(here == 1, rows[pl.ds(2 * half + 1, B, stride=4), :], filt).astype(bf16)
        padded = jnp.concatenate([jnp.zeros((B - R, B), bf16), weight], axis=0)
        for n in range(G):
            wide[:, n * B : (n + 1) * B] = padded[n * R : n * R + B]

        def turned(m):
            row = jnp.broadcast_to(rows[pl.ds(4 * m + 2 * half, 1), :], (B, B))
            return pltpu.roll(row, 1, 1, stride=1, stride_axis=0)

        after = jnp.zeros((B, B), f32)
        for m in reversed(range(B)):
            now = turned(m)
            block = jnp.where(inside, now, after).astype(bf16)
            hank[(m // R) * B : (m // R + 1) * B, (m % R) * B : (m % R + 1) * B] = block
            after = now
        sums[...] = jnp.dot(wide[...], hank[...], preferred_element_type=f32)
        spread[B * R :, :] = jnp.zeros((R * R, B), f32)
        for u in range(B):
            v, u0 = divmod(u, R)
            at = (G - 1 - v) * R
            spread[u * R : (u + 1) * R, :] = sums[at : at + R, u0 * B : (u0 + 1) * B]
        total = spread[pl.ds(0, B, stride=R), :]
        for r in range(1, R):
            total = total + spread[pl.ds((R + 1) * r, B, stride=R), :]
        results.append(total)
    both = results[0] + results[1]
    for half in range(2):
        out_ref[pl.ds(half, B, stride=2), :] = jnp.where(here == 1, both, results[half])


def finish_kernel(in_ref, cot_ref, gain_ref, grad_ref, filt_ref):
    here = lax.axis_index("ch")
    conv = in_ref[pl.ds(0, B, stride=2), :].T * (1.0 / B)
    grad_ref[...] = (gain_ref[...] * cot_ref[...].astype(f32) + conv).astype(bf16)
    totals = []
    for half in range(2):
        total = in_ref[pl.ds(16 * half + 1, 8, stride=2), :]
        for k in range(1, B // 16):
            total = total + in_ref[pl.ds(32 * k + 16 * half + 1, 8, stride=2), :]
        totals.append(total)
    filt_ref[...] = jnp.where(here == 1, totals[1], totals[0]) * (1.0 / B)


def on_device(activation, cotangent, filter_param, skip_gain):
    vmem = pl.BlockSpec(memory_space=pltpu.VMEM)
    axes = ("ctx", "ch")
    packed = pl.pallas_call(
        pack_kernel,
        out_shape=jax.ShapeDtypeStruct((4 * B, B), bf16),
        in_specs=[vmem] * 3,
        out_specs=vmem,
        scratch_shapes=[pltpu.VMEM((4 * B, B), f32)],
    )(activation, cotangent, filter_param.T)
    arrived = lax.all_to_all(packed.reshape(2 * B, 2, B), axes, 0, 0, tiled=True)
    partial = pl.pallas_call(
        correlate_kernel,
        out_shape=jax.ShapeDtypeStruct((2 * B, B), f32),
        in_specs=[vmem],
        out_specs=vmem,
        scratch_shapes=[
            pltpu.VMEM((4 * B, B), f32),
            pltpu.VMEM((B, G * B), bf16),
            pltpu.VMEM((G * B, R * B), bf16),
            pltpu.VMEM((B, R * B), f32),
            pltpu.VMEM((B * R + R * R, B), f32),
        ],
        compiler_params=pltpu.CompilerParams(vmem_limit_bytes=40 * 2**20),
    )(arrived.reshape(4 * B, B))
    back = lax.all_to_all(partial.reshape(2 * B, 1, B), axes, 0, 0, tiled=True)
    input_grad, filter_grad = pl.pallas_call(
        finish_kernel,
        out_shape=(jax.ShapeDtypeStruct((B, B), bf16), jax.ShapeDtypeStruct((8, B), f32)),
        in_specs=[vmem] * 3,
        out_specs=(vmem, vmem),
    )(back.reshape(2 * B, B), cotangent, skip_gain[None, :])
    return (input_grad, filter_grad.T)


def solution(mesh):
    return jax.shard_map(
        on_device,
        mesh=mesh,
        in_specs=(P("ctx", "ch"), P("ctx", "ch"), P("ctx", "ch"), P("ch")),
        out_specs=(P("ctx", "ch"), P("ctx", "ch")),
        check_vma=False,
    )
```

```python
import jax
import jax.numpy as jnp
from jax import lax
from jax.experimental import pallas as pl
from jax.experimental.pallas import tpu as pltpu
from jax.sharding import PartitionSpec as P

f32 = jnp.float32
bf16 = jnp.bfloat16
B = 128
R = 16
G = B // R
Q = B // 2


def pack_kernel(act_hbm, cot_hbm, filt_hbm, out_ref, act_ref, cot_ref, filt_ref, rows, sems):
    pairs = ((cot_hbm, cot_ref), (act_hbm, act_ref), (filt_hbm, filt_ref))
    copies = [pltpu.make_async_copy(src, dst, sems.at[n]) for n, (src, dst) in enumerate(pairs)]
    for copy in copies:
        copy.start()
    here = lax.axis_index("ch")
    at = lax.broadcasted_iota(jnp.int32, (B, B), 0)
    to = lax.broadcasted_iota(jnp.int32, (B, B), 1)
    flip = jnp.where(at + to == B - 1, 1.0, 0.0).astype(bf16)
    copies[0].wait()
    cot_t = cot_ref[...].astype(f32).T
    rows[pl.ds(0, B, stride=4), :] = cot_t
    rows[pl.ds(2, B, stride=4), :] = cot_t
    copies[1].wait()
    rows[pl.ds(3, B, stride=4), :] = lax.dot_general(
        act_ref[...], flip, (((0,), (0,)), ((), ())), preferred_element_type=f32
    )
    copies[2].wait()
    filt = jnp.dot(filt_ref[...], flip, preferred_element_type=f32)
    for h in range(B // 8):
        mine = jnp.where(here == h % 2, filt, 0.0)
        rows[pl.ds(32 * h + 1, 8, stride=4), :] = mine
    out_ref[...] = rows[...].astype(bf16)


def correlate_kernel(in_ref, cot_hbm, gain_hbm, out_ref, direct_ref, rows, wide, hank, sums, cot_ref, gain_ref, sems):
    copies = [
        pltpu.make_async_copy(cot_hbm, cot_ref, sems.at[0]),
        pltpu.make_async_copy(gain_hbm, gain_ref, sems.at[1]),
    ]
    for copy in copies:
        copy.start()
    here = lax.axis_index("ch")
    rows[...] = in_ref[...].astype(f32)
    q_at = lax.broadcasted_iota(jnp.int32, (Q, B), 0)
    b_at = lax.broadcasted_iota(jnp.int32, (Q, B), 1)
    inside = b_at <= q_at + Q
    low = lax.broadcasted_iota(jnp.int32, (R, B), 1) < Q
    low8 = lax.broadcasted_iota(jnp.int32, (G, B), 1) < Q
    filt = rows[pl.ds(1, B, stride=4), :] + rows[pl.ds(3, B, stride=4), :]
    sums[:, :, B:, :] = jnp.zeros((2, R, R, B), f32)
    first = []
    for half in range(2):
        plain = jnp.where(here == 1, rows[pl.ds(2 * half + 1, B, stride=4), :], filt)
        moved = pltpu.roll(plain, Q, 1).astype(bf16)
        plain = plain.astype(bf16)
        zero = jnp.zeros((R, B), bf16)
        for v in range(G):
            for pair in range(G // 2):
                at = [(2 * pair + e - v) * R for e in range(2)]
                for k in range(2):
                    source = (moved, plain) if k == 0 else (plain, moved)
                    even, odd = (source[e][at[e] : at[e] + R] if at[e] >= 0 else zero for e in range(2))
                    wide[k * B + v * R : k * B + (v + 1) * R, pair * B : (pair + 1) * B] = jnp.where(low, even, odd)

        def turned(m):
            row = jnp.broadcast_to(rows[pl.ds(4 * m + 2 * half, 1), :], (Q, B))
            return pltpu.roll(row, Q + 1, 1, stride=1, stride_axis=0).astype(bf16)

        after = [turned(R * (n + 1)) for n in range(G - 1)] + [jnp.zeros((Q, B), bf16)]
        for u in reversed(range(R)):
            for n in range(G):
                now = turned(R * n + u)
                hank[n * Q : (n + 1) * Q, u * B : (u + 1) * B] = jnp.where(inside, now, after[n])
                after[n] = now
            if u % 2 == 0:
                cols = slice(u * B, (u + 2) * B)
                product = jnp.dot(wide[...], hank[:, cols], preferred_element_type=f32)
                for k in range(2):
                    for e in range(2):
                        sums[k, u + e, :B] = product[k * B : (k + 1) * B, e * B : (e + 1) * B]

        def total(k, u):
            found = None
            for r in range(R):
                carry, col = divmod(u + r, R)
                piece = sums[k, col, pl.ds(R * carry + r, G, stride=R), :]
                found = piece if found is None else found + piece
            return found

        ahead = pltpu.roll(total(1, R), Q, 1)
        for u in reversed(range(R)):
            now = pltpu.roll(total(1, u), Q, 1)
            result = total(0, u) + jnp.where(low8, now, ahead)
            ahead = now
            if half == 0:
                first.append(result)
            else:
                other = first[R - 1 - u]
                both = other + result
                out_ref[pl.ds(2 * u, G, stride=2 * R), :] = jnp.where(here == 1, both, other)
                out_ref[pl.ds(2 * u + 1, G, stride=2 * R), :] = jnp.where(here == 1, both, result)
    for copy in copies:
        copy.wait()
    direct_ref[...] = gain_ref[...] * cot_ref[...].astype(f32)


def finish_kernel(in_ref, direct_ref, grad_ref, filt_ref):
    here = lax.axis_index("ch")
    conv = in_ref[pl.ds(0, B, stride=2), :].T * (1.0 / B)
    grad_ref[...] = (direct_ref[...] + conv).astype(bf16)
    totals = []
    for half in range(2):
        total = in_ref[pl.ds(16 * half + 1, 8, stride=2), :]
        for k in range(1, B // 16):
            total = total + in_ref[pl.ds(32 * k + 16 * half + 1, 8, stride=2), :]
        totals.append(total)
    filt_ref[...] = jnp.where(here == 1, totals[1], totals[0]) * (1.0 / B)


def on_device(activation, cotangent, filter_param, skip_gain):
    vmem = pl.BlockSpec(memory_space=pltpu.VMEM)
    hbm = pl.BlockSpec(memory_space=pltpu.HBM)
    axes = ("ctx", "ch")
    activation, cotangent, filters, gain = (
        pltpu.with_memory_space_constraint(x, pltpu.HBM)
        for x in (activation, cotangent, filter_param.T, skip_gain[None, :])
    )
    packed = pl.pallas_call(
        pack_kernel,
        out_shape=jax.ShapeDtypeStruct((4 * B, B), bf16),
        in_specs=[hbm] * 3,
        out_specs=vmem,
        scratch_shapes=[
            pltpu.VMEM((B, B), bf16),
            pltpu.VMEM((B, B), bf16),
            pltpu.VMEM((8, B), bf16),
            pltpu.VMEM((4 * B, B), f32),
            pltpu.SemaphoreType.DMA((3,)),
        ],
        compiler_params=pltpu.CompilerParams(vmem_limit_bytes=8 * 2**20),
    )(activation, cotangent, filters)
    arrived = lax.all_to_all(packed.reshape(2 * B, 2, B), axes, 0, 0, tiled=True)
    partial, direct = pl.pallas_call(
        correlate_kernel,
        out_shape=(jax.ShapeDtypeStruct((2 * B, B), f32), jax.ShapeDtypeStruct((B, B), f32)),
        in_specs=[vmem, hbm, hbm],
        out_specs=(vmem, vmem),
        scratch_shapes=[
            pltpu.VMEM((4 * B, B), f32),
            pltpu.VMEM((2 * B, G * Q), bf16),
            pltpu.VMEM((G * Q, R * B), bf16),
            pltpu.VMEM((2, R, B + R, B), f32),
            pltpu.VMEM((B, B), bf16),
            pltpu.VMEM((1, B), f32),
            pltpu.SemaphoreType.DMA((2,)),
        ],
        compiler_params=pltpu.CompilerParams(vmem_limit_bytes=24 * 2**20),
    )(arrived.reshape(4 * B, B), cotangent, gain)
    back = lax.all_to_all(partial.reshape(2 * B, 1, B), axes, 0, 0, tiled=True)
    input_grad, filter_grad = pl.pallas_call(
        finish_kernel,
        out_shape=(jax.ShapeDtypeStruct((B, B), bf16), jax.ShapeDtypeStruct((8, B), f32)),
        in_specs=[vmem, vmem],
        out_specs=(vmem, vmem),
        compiler_params=pltpu.CompilerParams(vmem_limit_bytes=8 * 2**20),
    )(back.reshape(2 * B, B), direct)
    return (input_grad, filter_grad.T)


def solution(mesh):
    return jax.shard_map(
        on_device,
        mesh=mesh,
        in_specs=(P("ctx", "ch"), P("ctx", "ch"), P("ctx", "ch"), P("ch")),
        out_specs=(P("ctx", "ch"), P("ctx", "ch")),
        check_vma=False,
    )
```

```python
import jax
import jax.numpy as jnp
from jax import lax
from jax.experimental import pallas as pl
from jax.experimental.pallas import tpu as pltpu
from jax.sharding import PartitionSpec as P

f32 = jnp.float32
bf16 = jnp.bfloat16
B = 128
R = 2
G = B // R
Q = 32
L = B // Q
E = 2 * L


def pack_kernel(
    act_hbm, cot_hbm, filt_hbm, gain_hbm, out_ref, direct_ref, act_ref, cot_ref, filt_ref, gain_ref, rows, sems
):
    pairs = ((cot_hbm, cot_ref), (act_hbm, act_ref), (filt_hbm, filt_ref), (gain_hbm, gain_ref))
    copies = [pltpu.make_async_copy(src, dst, sems.at[n]) for n, (src, dst) in enumerate(pairs)]
    for copy in copies:
        copy.start()
    here = lax.axis_index("ch")
    at = lax.broadcasted_iota(jnp.int32, (B, B), 0)
    to = lax.broadcasted_iota(jnp.int32, (B, B), 1)
    flip = jnp.where(at + to == B - 1, 1.0, 0.0).astype(bf16)
    copies[0].wait()
    cot = cot_ref[...].astype(f32)
    cot_t = cot.T
    rows[pl.ds(0, B, stride=4), :] = cot_t
    rows[pl.ds(2, B, stride=4), :] = cot_t
    copies[1].wait()
    rows[pl.ds(3, B, stride=4), :] = lax.dot_general(
        act_ref[...], flip, (((0,), (0,)), ((), ())), preferred_element_type=f32
    )
    copies[2].wait()
    filt = jnp.dot(filt_ref[...], flip, preferred_element_type=f32)
    for h in range(B // 8):
        mine = jnp.where(here == h % 2, filt, 0.0)
        rows[pl.ds(32 * h + 1, 8, stride=4), :] = mine
    out_ref[...] = rows[...].astype(bf16)
    copies[3].wait()
    direct_ref[...] = gain_ref[...] * cot


def correlate_kernel(in_ref, out_ref, rows, shifted, wide, hank, sums):
    here = lax.axis_index("ch")
    rows[...] = in_ref[...].astype(f32)
    q_at = lax.broadcasted_iota(jnp.int32, (Q, B), 0)
    b_at = lax.broadcasted_iota(jnp.int32, (Q, B), 1)
    inside = b_at <= q_at + B - Q
    to = lax.broadcasted_iota(jnp.int32, (B, B), 0)
    at = lax.broadcasted_iota(jnp.int32, (B, B), 1)
    swap = jnp.where(to + at - 2 * (to % 2) == B - 2, 1.0, 0.0).astype(bf16)
    group = at // Q
    lane = lax.broadcasted_iota(jnp.int32, (G, B), 1)
    filt = rows[pl.ds(1, B, stride=4), :] + rows[pl.ds(3, B, stride=4), :]
    shifted[:, B:, :] = jnp.zeros((L, 16, B), f32)
    sums[:, :, B:, :] = jnp.zeros((L, R, 8, B), f32)
    first = []
    for half in range(2):
        weight = jnp.where(here == 1, rows[pl.ds(2 * half + 1, B, stride=4), :], filt).astype(bf16)
        weight = jnp.dot(swap, weight, preferred_element_type=f32)
        for d in range(L):
            shifted[d, :B, :] = weight if d == 0 else pltpu.roll(weight, Q * d, 1)
        for k in range(L):
            for c in range(2):
                piece = None
                for j in range(L):
                    start = 2 * (E - 1) - 2 * L * c - 2 * j
                    taken = shifted[(j + k + 1) % L, start : start + B, :]
                    piece = taken if piece is None else jnp.where(group == j, taken, piece)
                piece = piece.astype(bf16)
                for i in range(B // 16):
                    wide[(L * i + k) * 16 : (L * i + k + 1) * 16, c * B : (c + 1) * B] = piece[16 * i : 16 * i + 16]

        def turned(m):
            row = jnp.broadcast_to(rows[pl.ds(4 * m + 2 * half, 1), :], (Q, B))
            return pltpu.roll(row, B - Q + 1, 1, stride=1, stride_axis=0).astype(bf16)

        after = jnp.zeros((Q, B), bf16)
        steps = G // E
        for e in reversed(range(steps)):
            slot = half * steps + e
            for m in reversed(range(R * E * e, R * E * (e + 1))):
                now = turned(m)
                n, u = divmod(m - R * E * e, R)
                hank[slot, n * Q : (n + 1) * Q, u * B : (u + 1) * B] = jnp.where(inside, now, after)
                after = now
            product = jnp.dot(wide[16 * L * (steps - 1 - e) :, :], hank[slot], preferred_element_type=f32)
            for i in range(e + 1):
                for k in range(L):
                    for u in range(R):
                        part = product[(L * i + k) * 16 : (L * i + k + 1) * 16, u * B : (u + 1) * B]
                        if e < steps - 1:
                            part = sums[k, u, 16 * i : 16 * i + 16, :] + part
                        sums[k, u, 16 * i : 16 * i + 16, :] = part

        def total(k, beta):
            found = None
            for r in range(R):
                carry, col = divmod(beta + r, R)
                piece = sums[k, col, pl.ds(R * carry + r, G, stride=R), :]
                found = piece if found is None else found + piece
            return found if k == 0 else pltpu.roll(found, B - Q * k, 1)

        results = [total(0, beta) for beta in range(R)]
        for k in range(1, L):
            turns = [total(k, beta) for beta in range(R + 1)]
            for beta in range(R):
                results[beta] = results[beta] + jnp.where(lane < B - Q * k, turns[beta], turns[beta + 1])
        if half == 0:
            first = results
            continue
        for beta in range(R):
            both = first[beta] + results[beta]
            for h, own in enumerate((first[beta], results[beta])):
                out_ref[pl.ds(2 * beta + h, G, stride=2 * R), :] = jnp.where(here == 1, both, own)


def finish_kernel(in_ref, direct_ref, grad_ref, filt_ref):
    here = lax.axis_index("ch")
    conv = in_ref[pl.ds(0, B, stride=2), :].T * (1.0 / B)
    grad_ref[...] = (direct_ref[...] + conv).astype(bf16)
    totals = []
    for half in range(2):
        total = in_ref[pl.ds(16 * half + 1, 8, stride=2), :]
        for k in range(1, B // 16):
            total = total + in_ref[pl.ds(32 * k + 16 * half + 1, 8, stride=2), :]
        totals.append(total)
    filt_ref[...] = jnp.where(here == 1, totals[1], totals[0]) * (1.0 / B)


def call_correlate(arrived):
    vmem = pl.BlockSpec(memory_space=pltpu.VMEM)
    return pl.pallas_call(
        correlate_kernel,
        out_shape=jax.ShapeDtypeStruct((2 * B, B), f32),
        in_specs=[vmem],
        out_specs=vmem,
        scratch_shapes=[
            pltpu.VMEM((4 * B, B), f32),
            pltpu.VMEM((L, B + 16, B), f32),
            pltpu.VMEM((L * B, E * Q), bf16),
            pltpu.VMEM((2 * G // E, E * Q, R * B), bf16),
            pltpu.VMEM((L, R, B + 8, B), f32),
        ],
        compiler_params=pltpu.CompilerParams(vmem_limit_bytes=24 * 2**20),
    )(arrived)


def on_device(activation, cotangent, filter_param, skip_gain):
    vmem = pl.BlockSpec(memory_space=pltpu.VMEM)
    hbm = pl.BlockSpec(memory_space=pltpu.HBM)
    axes = ("ctx", "ch")
    operands = (
        pltpu.with_memory_space_constraint(x, pltpu.HBM)
        for x in (activation, cotangent, filter_param.T, skip_gain[None, :])
    )
    packed, direct = pl.pallas_call(
        pack_kernel,
        out_shape=(jax.ShapeDtypeStruct((4 * B, B), bf16), jax.ShapeDtypeStruct((B, B), f32)),
        in_specs=[hbm] * 4,
        out_specs=(vmem, vmem),
        scratch_shapes=[
            pltpu.VMEM((B, B), bf16),
            pltpu.VMEM((B, B), bf16),
            pltpu.VMEM((8, B), bf16),
            pltpu.VMEM((1, B), f32),
            pltpu.VMEM((4 * B, B), f32),
            pltpu.SemaphoreType.DMA((4,)),
        ],
        compiler_params=pltpu.CompilerParams(vmem_limit_bytes=8 * 2**20),
    )(*operands)
    arrived = lax.all_to_all(packed.reshape(2 * B, 2, B), axes, 0, 0, tiled=True)
    partial = call_correlate(arrived.reshape(4 * B, B))
    back = lax.all_to_all(partial.reshape(2 * B, 1, B), axes, 0, 0, tiled=True)
    input_grad, filter_grad = pl.pallas_call(
        finish_kernel,
        out_shape=(jax.ShapeDtypeStruct((B, B), bf16), jax.ShapeDtypeStruct((8, B), f32)),
        in_specs=[vmem, vmem],
        out_specs=(vmem, vmem),
        compiler_params=pltpu.CompilerParams(vmem_limit_bytes=8 * 2**20),
    )(back.reshape(2 * B, B), direct)
    return (input_grad, filter_grad.T)


def solution(mesh):
    return jax.shard_map(
        on_device,
        mesh=mesh,
        in_specs=(P("ctx", "ch"), P("ctx", "ch"), P("ctx", "ch"), P("ch")),
        out_specs=(P("ctx", "ch"), P("ctx", "ch")),
        check_vma=False,
    )
```

```python
import jax
import jax.numpy as jnp
from jax import lax
from jax.experimental import pallas as pl
from jax.experimental.pallas import tpu as pltpu
from jax.sharding import PartitionSpec as P

f32 = jnp.float32
bf16 = jnp.bfloat16
B = 128
R = 2
G = B // R
Q = 32
L = B // Q
E = 2 * L


def pack_kernel(
    act_hbm, cot_hbm, filt_hbm, gain_hbm, out_ref, direct_ref, act_ref, cot_ref, filt_ref, gain_ref, rows, sems
):
    pairs = ((act_hbm, act_ref), (cot_hbm, cot_ref), (filt_hbm, filt_ref), (gain_hbm, gain_ref))
    copies = [pltpu.make_async_copy(src, dst, sems.at[n]) for n, (src, dst) in enumerate(pairs)]
    for copy in copies:
        copy.start()
    here = lax.axis_index("ch")
    at = lax.broadcasted_iota(jnp.int32, (B, B), 0)
    to = lax.broadcasted_iota(jnp.int32, (B, B), 1)
    flip = jnp.where(at + to == B - 1, 1.0, 0.0).astype(bf16)
    same = jnp.where(at == to, 1.0, 0.0).astype(bf16)
    for copy in copies:
        copy.wait()

    def turned(ref, onto):
        return lax.dot_general(ref[...], onto, (((0,), (0,)), ((), ())), preferred_element_type=f32)

    filt = jnp.dot(filt_ref[...], flip, preferred_element_type=f32)
    for h in range(B // 8):
        mine = jnp.where(here == h % 2, filt, 0.0)
        rows[pl.ds(32 * h + 1, 8, stride=4), :] = mine
    rows[pl.ds(3, B, stride=4), :] = turned(act_ref, flip)
    cot_t = turned(cot_ref, same)
    rows[pl.ds(0, B, stride=4), :] = cot_t
    rows[pl.ds(2, B, stride=4), :] = cot_t
    direct_ref[...] = gain_ref[...] * cot_ref[...].astype(f32)
    out_ref[...] = rows[...].astype(bf16)


def correlate_kernel(in_ref, out_ref, rows, shifted, wide, hank, sums):
    here = lax.axis_index("ch")
    rows[...] = in_ref[...].astype(f32)
    q_at = lax.broadcasted_iota(jnp.int32, (Q, B), 0)
    b_at = lax.broadcasted_iota(jnp.int32, (Q, B), 1)
    inside = b_at <= q_at + B - Q
    to = lax.broadcasted_iota(jnp.int32, (B, B), 0)
    at = lax.broadcasted_iota(jnp.int32, (B, B), 1)
    swap = jnp.where(to + at - 2 * (to % 2) == B - 2, 1.0, 0.0).astype(bf16)
    group = at // Q
    lane = lax.broadcasted_iota(jnp.int32, (G, B), 1)
    filt = rows[pl.ds(1, B, stride=4), :] + rows[pl.ds(3, B, stride=4), :]
    steps = G // E
    for half in range(2):
        shifted[half, :, B:, :] = jnp.zeros((L, 16, B), f32)
        sums[half, :, :, B:, :] = jnp.zeros((L, R, 8, B), f32)

    def prepare(half):
        weight = jnp.where(here == 1, rows[pl.ds(2 * half + 1, B, stride=4), :], filt).astype(bf16)
        weight = jnp.dot(swap, weight, preferred_element_type=f32)
        for d in range(L):
            shifted[half, d, :B, :] = weight if d == 0 else pltpu.roll(weight, Q * d, 1)
        for k in range(L):
            for c in range(2):
                piece = None
                for j in range(L):
                    start = 2 * (E - 1) - 2 * L * c - 2 * j
                    taken = shifted[half, (j + k + 1) % L, start : start + B, :]
                    piece = taken if piece is None else jnp.where(group == j, taken, piece)
                piece = piece.astype(bf16)
                for i in range(B // 16):
                    at_row = (L * i + k) * 16
                    wide[half, at_row : at_row + 16, c * B : (c + 1) * B] = piece[16 * i : 16 * i + 16]

    def turned(half, m):
        row = jnp.broadcast_to(rows[pl.ds(4 * m + 2 * half, 1), :], (Q, B))
        return pltpu.roll(row, B - Q + 1, 1, stride=1, stride_axis=0).astype(bf16)

    def spread(half, e, after):
        for m in reversed(range(R * E * e, R * E * (e + 1))):
            now = turned(half, m)
            n, u = divmod(m - R * E * e, R)
            hank[half, e, n * Q : (n + 1) * Q, u * B : (u + 1) * B] = jnp.where(inside, now, after)
            after = now
        return after

    def multiply(half, e):
        product = jnp.dot(wide[half, 16 * L * (steps - 1 - e) :, :], hank[half, e], preferred_element_type=f32)
        for i in range(e + 1):
            for k in range(L):
                for u in range(R):
                    part = product[(L * i + k) * 16 : (L * i + k + 1) * 16, u * B : (u + 1) * B]
                    if e < steps - 1:
                        part = sums[half, k, u, 16 * i : 16 * i + 16, :] + part
                    sums[half, k, u, 16 * i : 16 * i + 16, :] = part

    def total(half, k, beta):
        found = None
        for r in range(R):
            carry, col = divmod(beta + r, R)
            piece = sums[half, k, col, pl.ds(R * carry + r, G, stride=R), :]
            found = piece if found is None else found + piece
        return found if k == 0 else pltpu.roll(found, B - Q * k, 1)

    def combine(half):
        results = [total(half, 0, beta) for beta in range(R)]
        for k in range(1, L):
            turns = [total(half, k, beta) for beta in range(R + 1)]
            for beta in range(R):
                results[beta] = results[beta] + jnp.where(lane < B - Q * k, turns[beta], turns[beta + 1])
        return results

    prepare(0)
    prepare(1)
    after = [jnp.zeros((Q, B), bf16)] * 2
    for e in reversed(range(steps)):
        for half in range(2):
            after[half] = spread(half, e, after[half])
            multiply(half, e)
    found = [combine(half) for half in range(2)]
    for beta in range(R):
        both = found[0][beta] + found[1][beta]
        for h in range(2):
            out_ref[pl.ds(2 * beta + h, G, stride=2 * R), :] = jnp.where(here == 1, both, found[h][beta])


def finish_kernel(in_ref, direct_ref, grad_ref, filt_ref):
    here = lax.axis_index("ch")
    conv = in_ref[pl.ds(0, B, stride=2), :].T * (1.0 / B)
    grad_ref[...] = (direct_ref[...] + conv).astype(bf16)
    totals = []
    for half in range(2):
        total = in_ref[pl.ds(16 * half + 1, 8, stride=2), :]
        for k in range(1, B // 16):
            total = total + in_ref[pl.ds(32 * k + 16 * half + 1, 8, stride=2), :]
        totals.append(total)
    filt_ref[...] = jnp.where(here == 1, totals[1], totals[0]) * (1.0 / B)


def call_correlate(arrived):
    vmem = pl.BlockSpec(memory_space=pltpu.VMEM)
    return pl.pallas_call(
        correlate_kernel,
        out_shape=jax.ShapeDtypeStruct((2 * B, B), f32),
        in_specs=[vmem],
        out_specs=vmem,
        scratch_shapes=[
            pltpu.VMEM((4 * B, B), f32),
            pltpu.VMEM((2, L, B + 16, B), f32),
            pltpu.VMEM((2, L * B, E * Q), bf16),
            pltpu.VMEM((2, G // E, E * Q, R * B), bf16),
            pltpu.VMEM((2, L, R, B + 8, B), f32),
        ],
        compiler_params=pltpu.CompilerParams(vmem_limit_bytes=24 * 2**20),
    )(arrived)


def on_device(activation, cotangent, filter_param, skip_gain):
    vmem = pl.BlockSpec(memory_space=pltpu.VMEM)
    hbm = pl.BlockSpec(memory_space=pltpu.HBM)
    axes = ("ctx", "ch")
    operands = (
        pltpu.with_memory_space_constraint(x, pltpu.HBM)
        for x in (activation, cotangent, filter_param.T, skip_gain[None, :])
    )
    packed, direct = pl.pallas_call(
        pack_kernel,
        out_shape=(jax.ShapeDtypeStruct((4 * B, B), bf16), jax.ShapeDtypeStruct((B, B), f32)),
        in_specs=[hbm] * 4,
        out_specs=(vmem, vmem),
        scratch_shapes=[
            pltpu.VMEM((B, B), bf16),
            pltpu.VMEM((B, B), bf16),
            pltpu.VMEM((8, B), bf16),
            pltpu.VMEM((1, B), f32),
            pltpu.VMEM((4 * B, B), f32),
            pltpu.SemaphoreType.DMA((4,)),
        ],
        compiler_params=pltpu.CompilerParams(vmem_limit_bytes=8 * 2**20),
    )(*operands)
    arrived = lax.all_to_all(packed.reshape(2 * B, 2, B), axes, 0, 0, tiled=True)
    partial = call_correlate(arrived.reshape(4 * B, B))
    back = lax.all_to_all(partial.reshape(2 * B, 1, B), axes, 0, 0, tiled=True)
    input_grad, filter_grad = pl.pallas_call(
        finish_kernel,
        out_shape=(jax.ShapeDtypeStruct((B, B), bf16), jax.ShapeDtypeStruct((8, B), f32)),
        in_specs=[vmem, vmem],
        out_specs=(vmem, vmem),
        compiler_params=pltpu.CompilerParams(vmem_limit_bytes=8 * 2**20),
    )(back.reshape(2 * B, B), direct)
    return (input_grad, filter_grad.T)


def solution(mesh):
    return jax.shard_map(
        on_device,
        mesh=mesh,
        in_specs=(P("ctx", "ch"), P("ctx", "ch"), P("ctx", "ch"), P("ch")),
        out_specs=(P("ctx", "ch"), P("ctx", "ch")),
        check_vma=False,
    )
```

```python
import jax
import jax.numpy as jnp
from jax import lax
from jax.experimental import pallas as pl
from jax.experimental.pallas import tpu as pltpu
from jax.sharding import PartitionSpec as P

f32 = jnp.float32
bf16 = jnp.bfloat16
B = 128
R = 2
G = B // R
Q = 32
L = B // Q
E = 2 * L


def pack_kernel(flip_ref, same_ref, act_ref, cot_ref, filt_ref, gain_ref, out_ref, direct_ref, rows):
    here = lax.axis_index("ch")
    at = lax.broadcasted_iota(jnp.int32, (B, B), 0)
    to = lax.broadcasted_iota(jnp.int32, (B, B), 1)
    flip = flip_ref[...]
    same = same_ref[...]

    def turned(ref, onto):
        return lax.dot_general(ref[...], onto, (((0,), (0,)), ((), ())), preferred_element_type=f32)

    filt = jnp.dot(filt_ref[...], flip, preferred_element_type=f32)
    for h in range(B // 8):
        mine = jnp.where(here == h % 2, filt, 0.0)
        rows[pl.ds(32 * h + 1, 8, stride=4), :] = mine
    rows[pl.ds(3, B, stride=4), :] = turned(act_ref, flip)
    cot_t = turned(cot_ref, same)
    rows[pl.ds(0, B, stride=4), :] = cot_t
    rows[pl.ds(2, B, stride=4), :] = cot_t
    direct_ref[...] = gain_ref[...] * cot_ref[...].astype(f32)
    out_ref[...] = rows[...].astype(bf16)


def correlate_kernel(in_ref, out_ref, rows, shifted, wide, hank, sums):
    here = lax.axis_index("ch")
    rows[...] = in_ref[...].astype(f32)
    q_at = lax.broadcasted_iota(jnp.int32, (Q, B), 0)
    b_at = lax.broadcasted_iota(jnp.int32, (Q, B), 1)
    inside = b_at <= q_at + B - Q
    to = lax.broadcasted_iota(jnp.int32, (B, B), 0)
    at = lax.broadcasted_iota(jnp.int32, (B, B), 1)
    swap = jnp.where(to + at - 2 * (to % 2) == B - 2, 1.0, 0.0).astype(bf16)
    group = at // Q
    lane = lax.broadcasted_iota(jnp.int32, (8, B), 1)
    filt = rows[pl.ds(1, B, stride=4), :] + rows[pl.ds(3, B, stride=4), :]
    steps = G // E
    for half in range(2):
        shifted[half, :, B:, :] = jnp.zeros((L, 16, B), f32)
        sums[half, :, :, B:, :] = jnp.zeros((L, R, 8, B), f32)

    def prepare(half):
        weight = jnp.where(here == 1, rows[pl.ds(2 * half + 1, B, stride=4), :], filt).astype(bf16)
        weight = jnp.dot(swap, weight, preferred_element_type=f32)
        for d in range(L):
            shifted[half, d, :B, :] = weight if d == 0 else pltpu.roll(weight, Q * d, 1)
        for k in range(L):
            for c in range(2):
                piece = None
                for j in range(L):
                    start = 2 * (E - 1) - 2 * L * c - 2 * j
                    taken = shifted[half, (j + k + 1) % L, start : start + B, :]
                    piece = taken if piece is None else jnp.where(group == j, taken, piece)
                piece = piece.astype(bf16)
                for i in range(B // 16):
                    at_row = (L * i + k) * 16
                    wide[half, at_row : at_row + 16, c * B : (c + 1) * B] = piece[16 * i : 16 * i + 16]

    def turned(half, m):
        row = jnp.broadcast_to(rows[pl.ds(4 * m + 2 * half, 1), :], (Q, B))
        return pltpu.roll(row, B - Q + 1, 1, stride=1, stride_axis=0).astype(bf16)

    def spread(half, e, after):
        for m in reversed(range(R * E * e, R * E * (e + 1))):
            now = turned(half, m)
            n, u = divmod(m - R * E * e, R)
            hank[half, e, n * Q : (n + 1) * Q, u * B : (u + 1) * B] = jnp.where(inside, now, after)
            after = now
        return after

    def multiply(half, e):
        product = jnp.dot(wide[half, 16 * L * (steps - 1 - e) :, :], hank[half, e], preferred_element_type=f32)
        for i in range(e + 1):
            for k in range(L):
                for u in range(R):
                    part = product[(L * i + k) * 16 : (L * i + k + 1) * 16, u * B : (u + 1) * B]
                    if e < steps - 1:
                        part = sums[half, k, u, 16 * i : 16 * i + 16, :] + part
                    sums[half, k, u, 16 * i : 16 * i + 16, :] = part

    def total(half, e, k, beta):
        found = None
        for r in range(R):
            carry, col = divmod(beta + r, R)
            piece = sums[half, k, col, pl.ds(16 * e + R * carry + r, 8, stride=R), :]
            found = piece if found is None else found + piece
        return found if k == 0 else pltpu.roll(found, B - Q * k, 1)

    def combine(half, e):
        results = [total(half, e, 0, beta) for beta in range(R)]
        for k in range(1, L):
            turns = [total(half, e, k, beta) for beta in range(R + 1)]
            for beta in range(R):
                results[beta] = results[beta] + jnp.where(lane < B - Q * k, turns[beta], turns[beta + 1])
        return results

    def finish(e):
        found = [combine(half, e) for half in range(2)]
        for beta in range(R):
            both = found[0][beta] + found[1][beta]
            for h in range(2):
                at_row = 32 * e + 2 * beta + h
                out_ref[pl.ds(at_row, 8, stride=2 * R), :] = jnp.where(here == 1, both, found[h][beta])

    prepare(0)
    prepare(1)
    after = [jnp.zeros((Q, B), bf16)] * 2
    for e in reversed(range(steps)):
        for half in range(2):
            after[half] = spread(half, e, after[half])
            multiply(half, e)
    for e in reversed(range(steps)):
        finish(e)


def finish_kernel(in_ref, direct_ref, grad_ref, filt_ref):
    here = lax.axis_index("ch")
    conv = in_ref[pl.ds(0, B, stride=2), :].T * (1.0 / B)
    grad_ref[...] = (direct_ref[...] + conv).astype(bf16)
    totals = []
    for half in range(2):
        total = in_ref[pl.ds(16 * half + 1, 8, stride=2), :]
        for k in range(1, B // 16):
            total = total + in_ref[pl.ds(32 * k + 16 * half + 1, 8, stride=2), :]
        totals.append(total)
    filt_ref[...] = jnp.where(here == 1, totals[1], totals[0]) * (1.0 / B)


def call_correlate(arrived):
    vmem = pl.BlockSpec(memory_space=pltpu.VMEM)
    return pl.pallas_call(
        correlate_kernel,
        out_shape=jax.ShapeDtypeStruct((2 * B, B), f32),
        in_specs=[vmem],
        out_specs=vmem,
        scratch_shapes=[
            pltpu.VMEM((4 * B, B), f32),
            pltpu.VMEM((2, L, B + 16, B), f32),
            pltpu.VMEM((2, L * B, E * Q), bf16),
            pltpu.VMEM((2, G // E, E * Q, R * B), bf16),
            pltpu.VMEM((2, L, R, B + 8, B), f32),
        ],
        compiler_params=pltpu.CompilerParams(vmem_limit_bytes=24 * 2**20),
    )(arrived)


def on_device(activation, cotangent, filter_param, skip_gain):
    vmem = pl.BlockSpec(memory_space=pltpu.VMEM)
    axes = ("ctx", "ch")
    at = lax.broadcasted_iota(jnp.int32, (B, B), 0)
    to = lax.broadcasted_iota(jnp.int32, (B, B), 1)
    flip = jnp.where(at + to == B - 1, 1.0, 0.0).astype(bf16)
    same = jnp.where(at == to, 1.0, 0.0).astype(bf16)
    operands = (flip, same, activation, cotangent, filter_param.T, skip_gain[None, :])
    packed, direct = pl.pallas_call(
        pack_kernel,
        out_shape=(jax.ShapeDtypeStruct((4 * B, B), bf16), jax.ShapeDtypeStruct((B, B), f32)),
        in_specs=[vmem] * 6,
        out_specs=(vmem, vmem),
        scratch_shapes=[
            pltpu.VMEM((4 * B, B), f32),
        ],
        compiler_params=pltpu.CompilerParams(vmem_limit_bytes=8 * 2**20),
    )(*operands)
    arrived = lax.all_to_all(packed.reshape(2 * B, 2, B), axes, 0, 0, tiled=True)
    partial = call_correlate(arrived.reshape(4 * B, B))
    back = lax.all_to_all(partial.reshape(2 * B, 1, B), axes, 0, 0, tiled=True)
    input_grad, filter_grad = pl.pallas_call(
        finish_kernel,
        out_shape=(jax.ShapeDtypeStruct((B, B), bf16), jax.ShapeDtypeStruct((8, B), f32)),
        in_specs=[vmem, vmem],
        out_specs=(vmem, vmem),
        compiler_params=pltpu.CompilerParams(vmem_limit_bytes=8 * 2**20),
    )(back.reshape(2 * B, B), direct)
    return (input_grad, filter_grad.T)


def solution(mesh):
    return jax.shard_map(
        on_device,
        mesh=mesh,
        in_specs=(P("ctx", "ch"), P("ctx", "ch"), P("ctx", "ch"), P("ch")),
        out_specs=(P("ctx", "ch"), P("ctx", "ch")),
        check_vma=False,
    )
```
